32 devices in a mesh: pipe: 2 (over x), dp: 16 (over z, y, core).
Axes of the slice: x: 2, y: 2, z: 4, core: 2. Of those that a mesh axis runs over, the one named last changes fastest.
Arguments:
- tokens: bfloat16 [512, 6144], P(('pipe', 'dp')), may hold values from -6 to 6
- cotangent: bfloat16 [512, 6144], P(('pipe', 'dp')), may hold values from -6 to 6
- norm_gain: float32 [2, 6144], P('pipe'), may hold values from 0.5 to 1.5
- up_blocks: float32 [2, 4, 96, 384], P('pipe'), may hold values from -0.625 to 0.625
- down_blocks: float32 [2, 4, 96, 384], P('pipe'), may hold values from -0.3125 to 0.3125
- up_left: float32 [2, 8, 6144], P('pipe'), may hold values from -0.078125 to 0.078125
- up_right: float32 [2, 8, 24576], P('pipe'), may hold values from -2 to 2
- down_left: float32 [2, 8, 24576], P('pipe'), may hold values from -0.0390625 to 0.0390625
- down_right: float32 [2, 8, 6144], P('pipe'), may hold values from -2 to 2
- block_pattern: int32 [2, 2, 2, 4], P('pipe'), may hold values from 0 to 63, as said below
- rank_used: int32 [2, 2], P('pipe'), may hold values from 1 to 8
Outputs:
- final_tokens: bfloat16 [512, 6144], P(('pipe', 'dp'))
- input_gradient: bfloat16 [512, 6144], P(('pipe', 'dp'))
- grad_up_blocks: float32 [2, 4, 96, 384], P('pipe', None, None, 'dp')
- grad_down_blocks: float32 [2, 4, 96, 384], P('pipe', None, None, 'dp')
- grad_up_left: float32 [2, 8, 6144], P('pipe', None, 'dp')
- grad_up_right: float32 [2, 8, 24576], P('pipe', None, 'dp')
- grad_down_left: float32 [2, 8, 24576], P('pipe', None, 'dp')
- grad_down_right: float32 [2, 8, 6144], P('pipe', None, 'dp')
- grad_gain: float32 [2, 6144], P('pipe', 'dp')
The draws below stay inside these ranges and needn't reach their ends.
Inputs may be any that keep to these rules, and one draw needn't show every extreme that they name: block_pattern[l, p, 1, k] is block_pattern[l, p, 0, k] with exactly one of its 6 bits flipped (a butterfly pair); pairs may repeat.
All inputs are finite; a program needn't handle non-finite values.
Results may differ from the reference program's by a relative error of at most 0.0052.
Values may be sent and summed in bfloat16 or wider, within the bound.
A program may use at most 128 MiB of HBM per device.

```python
import math
import jax
import jax.numpy as jnp
from jax import lax

D = 6144
FF = 24576
NB = 64
LEVELS = 6
NBLK = 4
RANK = 8
LAYERS = 2
BD = 96
BF = 384
TOKENS = 512


def draw_block_pattern(key, part):
    key_rows, key_levels = jax.random.split(jax.random.fold_in(key, 7))
    row_blocks = jax.random.randint(key_rows, (LAYERS, 2, NBLK), 0, NB, dtype=jnp.int32)
    row_blocks = row_blocks.at[:, :, 0].set(NB - 1).at[:, :, 1].set(0)
    levels = jax.random.randint(key_levels, (LAYERS, 2, NBLK), 0, LEVELS, dtype=jnp.int32)
    col_blocks = jnp.bitwise_xor(row_blocks, jnp.left_shift(jnp.ones_like(levels), levels))
    return jnp.stack([row_blocks, col_blocks], axis=2)


def draw_rank_used(key, part):
    rank_draw = jax.random.randint(jax.random.fold_in(key, 11), (LAYERS, 2), 1, RANK + 1, dtype=jnp.int32)
    return rank_draw.at[0, 0].set(RANK)


def strengthened(entries, rng, source, target, shards_of, factor):
    def block_of(position):
        return (jnp.arange(entries.shape[position]) // (entries.shape[position] // shards_of)).reshape((-1,) + (1,) * (entries.ndim - 1 - position))

    near = jax.random.permutation(rng, shards_of)[block_of(target)]
    other_side = (block_of(target) + shards_of // 2) % shards_of
    return jnp.where((block_of(source) == near) | (block_of(source) == other_side), factor * entries, entries)


def block_levels(stream_key, extent, shards, low, high):
    level = 1.0
    for dim, shards_of in shards:
        draws = jax.random.uniform(jax.random.fold_in(jax.random.fold_in(stream_key, 6), dim), (shards_of,), jnp.float32, low / len(shards), high / len(shards))
        level = level * jnp.repeat(jnp.exp(draws), extent[dim] // shards_of).reshape((-1,) + (1,) * (len(extent) - 1 - dim))
    return level


def scatter_about(rng, extent, spread, reach, cuts=(), kind=jnp.bfloat16):
    entries = spread * jax.random.normal(rng, extent, jnp.float32)
    if cuts:
        entries = entries * block_levels(rng, extent, cuts, -0.22, 0.18)
    return jnp.clip(entries, -reach, reach).astype(kind)


def bell_draw_with(key, shape, spread, limit, shards, heavy, held_as=jnp.bfloat16):
    drawn = spread * jax.random.normal(key, shape, jnp.float32)
    if shards:
        drawn = drawn * block_levels(key, shape, shards, -0.22, 0.18)
    return jnp.clip(strengthened(drawn, jax.random.fold_in(key, 3), *heavy), -limit, limit).astype(held_as)


def setup_inputs(seed: int = 0) -> dict:
    streams_of = jax.random.split(jax.random.key(seed), 12)
    return {
        "tokens": scatter_about(streams_of[0], (TOKENS, D), 1.0, 6.0, ((0, 32),)),
        "cotangent": bell_draw_with(streams_of[1], (TOKENS, D), 1.0, 6.0, ((0, 32),), (0, 1, 32, 2.75)),
        "norm_gain": jnp.clip(1.0 + 0.1 * jax.random.normal(streams_of[2], (LAYERS, D), jnp.float32), 0.5, 1.5),
        "up_blocks": scatter_about(streams_of[3], (LAYERS, NBLK, BD, BF), BD ** -0.5, 0.625, ((0, 2),), jnp.float32),
        "down_blocks": scatter_about(streams_of[4], (LAYERS, NBLK, BD, BF), BF ** -0.5, 0.3125, ((0, 2),), jnp.float32),
        "up_left": scatter_about(streams_of[5], (LAYERS, RANK, D), D ** -0.5, 0.078125, ((0, 2),), jnp.float32),
        "up_right": scatter_about(streams_of[6], (LAYERS, RANK, FF), RANK ** -0.5, 2.0, ((0, 2),), jnp.float32),
        "down_left": scatter_about(streams_of[7], (LAYERS, RANK, FF), FF ** -0.5, 0.0390625, ((0, 2),), jnp.float32),
        "down_right": scatter_about(streams_of[8], (LAYERS, RANK, D), RANK ** -0.5, 2.0, ((0, 2),), jnp.float32),
        "block_pattern": draw_block_pattern(jax.random.fold_in(streams_of[11], 71), 0),
        "rank_used": draw_rank_used(jax.random.fold_in(streams_of[11], 71), 0),
    }


precise = lax.Precision.HIGHEST

def gelu_tanh(value):
    return 0.5 * value * (1.0 + jnp.tanh(0.7978845608028654 * (value + 0.044715 * value * value * value)))

def layer_apply(act, params, pattern, ranks):
    up_blocks, down_blocks, up_left, up_right, down_left, down_right, gain = params
    token_count = act.shape[0]
    feature_width = act.shape[1]
    block_feat = up_blocks.shape[1]
    block_hidden = up_blocks.shape[2]
    group_count = feature_width // block_feat
    hidden_width = up_right.shape[1]
    rank_index = jnp.arange(up_left.shape[0], dtype=jnp.int32)
    up_mask = jnp.where(rank_index < ranks[0], 1.0, 0.0).astype(jnp.float32)
    down_mask = jnp.where(rank_index < ranks[1], 1.0, 0.0).astype(jnp.float32)
    mean_square = lax.optimization_barrier(jnp.mean(act * act, axis=1, keepdims=True))
    normed = act * lax.rsqrt(mean_square + 1e-05) * gain
    pieces = jnp.take(normed.reshape(token_count, group_count, block_feat), pattern[0, 0], axis=1)
    up_parts = jnp.einsum('rkd,kdf->rkf', pieces, up_blocks, precision=precise)
    low_coeff = jnp.einsum('rd,qd->rq', normed, up_left, precision=precise) * up_mask
    hidden = jnp.einsum('rq,qf->rf', low_coeff, up_right, precision=precise)
    hidden = hidden.reshape(token_count, group_count, block_hidden).at[:, pattern[0, 1]].add(up_parts)
    hidden = gelu_tanh(hidden)
    hidden_pieces = jnp.take(hidden, pattern[1, 0], axis=1)
    down_parts = jnp.einsum('rkf,kdf->rkd', hidden_pieces, down_blocks, precision=precise)
    flat_hidden = hidden.reshape(token_count, hidden_width)
    low_down = jnp.einsum('rf,qf->rq', flat_hidden, down_left, precision=precise) * down_mask
    branch = jnp.einsum('rq,qd->rd', low_down, down_right, precision=precise)
    branch = branch.reshape(token_count, group_count, block_feat).at[:, pattern[1, 1]].add(down_parts)
    return act + branch.reshape(token_count, feature_width)

def reference(tokens, cotangent, norm_gain, up_blocks, down_blocks, up_left, up_right, down_left, down_right, block_pattern, rank_used):
    weights = []
    for layer_index in range(LAYERS):
        weights.append((up_blocks[layer_index], down_blocks[layer_index], up_left[layer_index], up_right[layer_index], down_left[layer_index], down_right[layer_index], norm_gain[layer_index]))
    block_size = math.gcd(TOKENS, 512)
    blocks_total = TOKENS // block_size
    token_blocks = tokens.reshape(blocks_total, block_size, D)
    grad_blocks = cotangent.reshape(blocks_total, block_size, D)

    def one_block(totals, inputs):
        rows_in, rows_grad = inputs
        current = rows_in
        layer_inputs = []
        for layer_index in range(LAYERS):
            widened = current.astype(jnp.float32)
            layer_inputs.append(widened)
            output = layer_apply(widened, weights[layer_index], block_pattern[layer_index], rank_used[layer_index])
            current = lax.optimization_barrier(output.astype(jnp.bfloat16))
        final_rows = current
        upstream = rows_grad.astype(jnp.float32)
        new_totals = list(totals)
        rounded = rows_grad
        for layer_index in reversed(range(LAYERS)):
            pattern_here = block_pattern[layer_index]
            ranks_here = rank_used[layer_index]

            def mapped(act, params, pattern_here=pattern_here, ranks_here=ranks_here):
                return layer_apply(act, params, pattern_here, ranks_here)
            unused, pull = jax.vjp(mapped, layer_inputs[layer_index], weights[layer_index])
            act_grad, param_grads = pull(upstream)
            new_totals[layer_index] = tuple((old + new for old, new in zip(totals[layer_index], param_grads)))
            rounded = lax.optimization_barrier(act_grad.astype(jnp.bfloat16))
            upstream = rounded.astype(jnp.float32)
        return (tuple(new_totals), (final_rows, rounded))
    initial = tuple((tuple((jnp.zeros_like(item) for item in weights[layer_index])) for layer_index in range(LAYERS)))
    totals, outputs = lax.scan(one_block, initial, (token_blocks, grad_blocks))
    final_tokens = outputs[0].reshape(TOKENS, D)
    input_gradient = outputs[1].reshape(TOKENS, D)
    factor = 1.0 / math.sqrt(TOKENS)
    stacked = [jnp.stack([totals[layer_index][which] for layer_index in range(LAYERS)]) * factor for which in range(7)]
    return (final_tokens, input_gradient, stacked[0], stacked[1], stacked[2], stacked[3], stacked[4], stacked[5], stacked[6])
```

```python
import math

import jax
import jax.numpy as jnp
from jax import lax
from jax.sharding import PartitionSpec as P

precise = lax.Precision.HIGHEST


def from_behind(block, axis, distance):
    devices = range(lax.axis_size(axis))
    route = [(i - distance, i) for i in devices if i - distance in devices]
    return lax.ppermute(block, axis, route)


def gelu_tanh(value):
    return (
        0.5
        * value
        * (1.0 + jnp.tanh(0.7978845608028654 * (value + 0.044715 * value * value * value)))
    )


def selector(indices, group_count):
    groups = jnp.arange(group_count, dtype=jnp.int32)
    return jnp.where(indices[:, None] == groups[None, :], 1.0, 0.0).astype(jnp.float32)


def layer_apply(act, params, pattern, ranks):
    up_blocks, down_blocks, up_left, up_right, down_left, down_right, gain = params
    token_count = act.shape[0]
    feature_width = act.shape[1]
    block_feat = up_blocks.shape[1]
    block_hidden = up_blocks.shape[2]
    group_count = feature_width // block_feat
    hidden_width = up_right.shape[1]
    rank_index = jnp.arange(up_left.shape[0], dtype=jnp.int32)
    up_mask = jnp.where(rank_index < ranks[0], 1.0, 0.0).astype(jnp.float32)
    down_mask = jnp.where(rank_index < ranks[1], 1.0, 0.0).astype(jnp.float32)
    up_source = selector(pattern[0, 0], group_count)
    up_target = selector(pattern[0, 1], group_count)
    down_source = selector(pattern[1, 0], group_count)
    down_target = selector(pattern[1, 1], group_count)
    mean_square = jnp.mean(act * act, axis=1, keepdims=True)
    normed = act * lax.rsqrt(mean_square + 1e-05) * gain
    pieces = jnp.einsum(
        "rgd,kg->rkd",
        normed.reshape(token_count, group_count, block_feat),
        up_source,
        precision=precise,
    )
    up_parts = jnp.einsum("rkd,kdf->rkf", pieces, up_blocks, precision=precise)
    low_coeff = jnp.einsum("rd,qd->rq", normed, up_left, precision=precise) * up_mask
    hidden = jnp.einsum("rq,qf->rf", low_coeff, up_right, precision=precise).reshape(
        token_count, group_count, block_hidden
    )
    hidden = gelu_tanh(hidden + jnp.einsum("rkf,kg->rgf", up_parts, up_target, precision=precise))
    hidden_pieces = jnp.einsum("rgf,kg->rkf", hidden, down_source, precision=precise)
    down_parts = jnp.einsum("rkf,kdf->rkd", hidden_pieces, down_blocks, precision=precise)
    flat_hidden = hidden.reshape(token_count, hidden_width)
    low_down = jnp.einsum("rf,qf->rq", flat_hidden, down_left, precision=precise) * down_mask
    branch = jnp.einsum("rq,qd->rd", low_down, down_right, precision=precise)
    placed = jnp.einsum("rkd,kg->rgd", down_parts, down_target, precision=precise).reshape(
        token_count, feature_width
    )
    return act + branch + placed


def shards(
    tokens,
    cotangent,
    norm_gain,
    up_blocks,
    down_blocks,
    up_left,
    up_right,
    down_left,
    down_right,
    block_pattern,
    rank_used,
):
    sections = lax.axis_size("pipe")
    replicas = lax.axis_size("dp")
    section_index = lax.axis_index("pipe")
    last_section = sections - 1
    micro_rows = tokens.shape[0]
    feature_width = tokens.shape[1]
    section_params = (
        up_blocks[0],
        down_blocks[0],
        up_left[0],
        up_right[0],
        down_left[0],
        down_right[0],
        norm_gain[0],
    )
    section_pattern = block_pattern[0]
    section_ranks = rank_used[0]
    turns = 2 * sections - 1

    def mapped(act, params):
        return layer_apply(act, params, section_pattern, section_ranks)

    def forward_apply(source):
        return mapped(source.astype(jnp.float32), section_params).astype(jnp.bfloat16)

    def forward_spare(source):
        return jnp.zeros_like(source)

    forward_store = tokens
    backward_store = cotangent

    def place_result(handoff_store, emit_rows, result):
        return jnp.where(emit_rows, result, handoff_store)

    def forward_compute(step_index, incoming, handoff_store, saved_inputs):
        micro_index = step_index - section_index
        active = jnp.logical_and(micro_index >= 0, micro_index < sections)
        slot_index = jnp.clip(micro_index, 0, last_section)
        first_rows = handoff_store
        source = jnp.where(section_index == 0, first_rows, incoming)
        result = lax.cond(active, forward_apply, forward_spare, source)
        kept = lax.dynamic_index_in_dim(saved_inputs, slot_index, 0, keepdims=False)
        saved_inputs = lax.dynamic_update_index_in_dim(
            saved_inputs, jnp.where(active, source, kept), slot_index, 0
        )
        emit_rows = jnp.logical_and(active, section_index == last_section)
        handoff_store = place_result(handoff_store, emit_rows, result)
        return (result, handoff_store, saved_inputs)

    def forward_turn(step_index, loop_state):
        incoming, handoff_store, saved_inputs = loop_state
        result, handoff_store, saved_inputs = forward_compute(
            step_index, incoming, handoff_store, saved_inputs
        )
        incoming = from_behind(result, "pipe", 1)
        handoff_store = from_behind(handoff_store, "pipe", -1)
        return (incoming, handoff_store, saved_inputs)

    saved_start = jnp.zeros((sections, micro_rows, feature_width), jnp.bfloat16)
    zero_rows = jnp.zeros((micro_rows, feature_width), jnp.bfloat16)
    loop_state = lax.fori_loop(0, turns - 1, forward_turn, (zero_rows, forward_store, saved_start))
    unused, forward_store, saved_inputs = forward_compute(
        turns - 1, loop_state[0], loop_state[1], loop_state[2]
    )
    zero_grads = tuple((jnp.zeros_like(item) for item in section_params))

    def backward_apply(operands):
        source, upstream, totals = operands
        unused_out, pull = jax.vjp(mapped, source.astype(jnp.float32), section_params)
        act_grad, param_grads = pull(upstream.astype(jnp.float32))
        new_totals = tuple((old + new for old, new in zip(totals, param_grads)))
        return (act_grad.astype(jnp.bfloat16), new_totals)

    def backward_spare(operands):
        return (jnp.zeros_like(operands[0]), operands[2])

    def backward_compute(step_index, incoming, handoff_store, totals):
        micro_index = 2 * last_section - step_index - section_index
        active = jnp.logical_and(micro_index >= 0, micro_index < sections)
        slot_index = jnp.clip(micro_index, 0, last_section)
        top_rows = handoff_store
        upstream = jnp.where(section_index == last_section, top_rows, incoming)
        source = lax.dynamic_index_in_dim(saved_inputs, slot_index, 0, keepdims=False)
        result, totals = lax.cond(
            active, backward_apply, backward_spare, (source, upstream, totals)
        )
        emit_rows = jnp.logical_and(active, section_index == 0)
        handoff_store = place_result(handoff_store, emit_rows, result)
        return (result, handoff_store, totals)

    def backward_turn(step_index, loop_state):
        incoming, handoff_store, totals = loop_state
        result, handoff_store, totals = backward_compute(
            step_index, incoming, handoff_store, totals
        )
        incoming = from_behind(result, "pipe", -1)
        handoff_store = from_behind(handoff_store, "pipe", 1)
        return (incoming, handoff_store, totals)

    loop_state = lax.fori_loop(0, turns - 1, backward_turn, (zero_rows, backward_store, zero_grads))
    unused, backward_store, totals = backward_compute(
        turns - 1, loop_state[0], loop_state[1], loop_state[2]
    )
    expanded = tuple((item[None] for item in totals))
    summed = (
        lax.psum_scatter(expanded[0], "dp", scatter_dimension=3, tiled=True),
        lax.psum_scatter(expanded[1], "dp", scatter_dimension=3, tiled=True),
        lax.psum_scatter(expanded[2], "dp", scatter_dimension=2, tiled=True),
        lax.psum_scatter(expanded[3], "dp", scatter_dimension=2, tiled=True),
        lax.psum_scatter(expanded[4], "dp", scatter_dimension=2, tiled=True),
        lax.psum_scatter(expanded[5], "dp", scatter_dimension=2, tiled=True),
        lax.psum_scatter(expanded[6], "dp", scatter_dimension=1, tiled=True),
    )
    factor = 1.0 / math.sqrt(micro_rows * sections * replicas)
    scaled = [item * factor for item in summed]
    return (
        forward_store,
        backward_store,
        scaled[0],
        scaled[1],
        scaled[2],
        scaled[3],
        scaled[4],
        scaled[5],
        scaled[6],
    )


def matmul(a, b, ca, cb):
    return lax.dot_general(
        a, b, (((ca,), (cb,)), ((), ())),
        precision=lax.Precision.HIGH, preferred_element_type=jnp.float32,
    )


def take_block(rows, index, width):
    return lax.dynamic_slice_in_dim(rows, index * width, width, 1)


def add_block(rows, part, index):
    width = part.shape[1]
    old = lax.dynamic_slice_in_dim(rows, index * width, width, 1)
    return lax.dynamic_update_slice_in_dim(rows, old + part, index * width, 1)


def masks(ranks, count):
    rank_index = jnp.arange(count, dtype=jnp.int32)
    return (
        jnp.where(rank_index < ranks[0], 1.0, 0.0).astype(jnp.float32),
        jnp.where(rank_index < ranks[1], 1.0, 0.0).astype(jnp.float32),
    )


def forward_pass(rows, params, pattern, ranks):
    up_blocks, down_blocks, up_left, up_right, down_left, down_right, gain = params
    act = rows.astype(jnp.float32)
    blocks, feat, hid = up_blocks.shape
    up_mask, down_mask = masks(ranks, up_left.shape[0])
    scale = lax.rsqrt(jnp.mean(act * act, axis=1, keepdims=True) + 1e-05)
    normed = act * scale * gain
    low = matmul(normed, up_left, 1, 1) * up_mask
    pre = matmul(low, up_right, 1, 0)
    for k in range(blocks):
        part = matmul(take_block(normed, pattern[0, 0, k], feat), up_blocks[k], 1, 0)
        pre = add_block(pre, part, pattern[0, 1, k])
    hidden = gelu_tanh(pre)
    low_down = matmul(hidden, down_left, 1, 1) * down_mask
    out = act + matmul(low_down, down_right, 1, 0)
    for k in range(blocks):
        part = matmul(take_block(hidden, pattern[1, 0, k], hid), down_blocks[k], 1, 1)
        out = add_block(out, part, pattern[1, 1, k])
    return out.astype(jnp.bfloat16), (scale, low, pre, low_down)


def backward_pass(rows, upstream, saved, params, pattern, ranks, replicas):
    up_blocks, down_blocks, up_left, up_right, down_left, down_right, gain = params
    scale, low, pre, low_down = saved
    act = rows.astype(jnp.float32)
    grad = upstream.astype(jnp.float32)
    blocks, feat, hid = up_blocks.shape
    up_mask, down_mask = masks(ranks, up_left.shape[0])
    unit = act * scale
    normed = unit * gain
    tanh = jnp.tanh(0.7978845608028654 * (pre + 0.044715 * pre * pre * pre))
    hidden = 0.5 * pre * (1.0 + tanh)
    slope = 0.5 * (1.0 + tanh) + 0.5 * pre * (1.0 - tanh * tanh) * (
        0.7978845608028654 * (1.0 + 3.0 * 0.044715 * pre * pre)
    )
    d_low_down = matmul(grad, down_right, 1, 1) * down_mask
    d_hidden = matmul(d_low_down, down_left, 1, 0)
    g_down = []
    for k in range(blocks):
        piece = take_block(grad, pattern[1, 1, k], feat)
        d_hidden = add_block(d_hidden, matmul(piece, down_blocks[k], 1, 0), pattern[1, 0, k])
        g_down.append(matmul(take_block(hidden, pattern[1, 0, k], hid), piece, 0, 0))
    d_pre = d_hidden * slope
    d_low = matmul(d_pre, up_right, 1, 1) * up_mask
    d_normed = matmul(d_low, up_left, 1, 0)
    g_up = []
    for k in range(blocks):
        piece = take_block(d_pre, pattern[0, 1, k], hid)
        d_normed = add_block(d_normed, matmul(piece, up_blocks[k], 1, 1), pattern[0, 0, k])
        g_up.append(matmul(piece, take_block(normed, pattern[0, 0, k], feat), 0, 0))
    scaled = d_normed * gain
    act_grad = grad + scale * (scaled - unit * jnp.mean(scaled * unit, axis=1, keepdims=True))
    g_gain = jnp.sum(d_normed * unit, axis=0)

    def by_share(g):
        return g.reshape(g.shape[0], replicas, -1).transpose(1, 0, 2)

    def block_share(g):
        whole = jnp.concatenate(g, axis=1)
        eighths = whole.reshape(replicas, -1, 8, whole.shape[1]).transpose(0, 2, 1, 3)
        return eighths.reshape(replicas, 8, -1)

    gain_rows = jnp.pad(g_gain.reshape(replicas, 1, -1), ((0, 0), (0, 7), (0, 0)))
    packed = jnp.concatenate(
        [
            by_share(matmul(low, d_pre, 0, 0)),
            by_share(matmul(d_low_down, hidden, 0, 0)),
            by_share(matmul(d_low, normed, 0, 0)),
            by_share(matmul(low_down, grad, 0, 0)),
            block_share(g_up),
            block_share(g_down),
            gain_rows,
        ],
        axis=2,
    )
    return act_grad.astype(jnp.bfloat16), packed


def reduce_shares(packed):
    return lax.psum_scatter(packed, "dp", scatter_dimension=0, tiled=False)


def two_sections(
    tokens,
    cotangent,
    norm_gain,
    up_blocks,
    down_blocks,
    up_left,
    up_right,
    down_left,
    down_right,
    block_pattern,
    rank_used,
):
    replicas = lax.axis_size("dp")
    section = lax.axis_index("pipe")
    count, width = tokens.shape
    params = (
        up_blocks[0],
        down_blocks[0],
        up_left[0],
        up_right[0],
        down_left[0],
        down_right[0],
        norm_gain[0],
    )
    pattern = block_pattern[0]
    ranks = rank_used[0]
    forth, back = [(0, 1)], [(1, 0)]
    first = jnp.concatenate([tokens, lax.ppermute(tokens, "pipe", back)], axis=0)
    top = jnp.concatenate([lax.ppermute(cotangent, "pipe", forth), cotangent], axis=0)

    def run(rows):
        return forward_pass(rows, params, pattern, ranks)

    def skip_forward(rows):
        return jax.tree.map(lambda t: jnp.zeros(t.shape, t.dtype), jax.eval_shape(run, rows))

    result, saved = lax.cond(section == 0, run, skip_forward, first)
    second = lax.ppermute(result, "pipe", forth)

    def last(operands):
        rows, upstream = operands
        out, kept = run(rows)
        below, packed = backward_pass(rows, upstream, kept, params, pattern, ranks, replicas)
        return out, below, packed

    def skip_last(operands):
        return jax.tree.map(lambda t: jnp.zeros(t.shape, t.dtype), jax.eval_shape(last, operands))

    final, below, packed = lax.cond(section == 1, last, skip_last, (second, top))
    from_above = lax.ppermute(below, "pipe", back)
    final_early = lax.ppermute(final[:count], "pipe", back)

    def first_back(operands):
        upstream, kept, unused = operands
        return backward_pass(first, upstream, kept, params, pattern, ranks, replicas)

    def skip_back(operands):
        return operands[0], operands[2]

    bottom, packed = lax.cond(section == 0, first_back, skip_back, (from_above, saved, packed))
    bottom_late = lax.ppermute(bottom[count:], "pipe", forth)
    final_tokens = jnp.where(section == 0, final_early, final[count:])
    input_gradient = jnp.where(section == 0, bottom[:count], bottom_late)
    factor = 1.0 / math.sqrt(count * 2 * replicas)
    share = reduce_shares(packed) * factor
    blocks, feat, hid = params[0].shape
    hidden_share = params[3].shape[1] // replicas
    width_share = width // replicas
    block_columns = hid // replicas // 8 * blocks * feat
    pieces = []
    start = 0
    for extent in (hidden_share, hidden_share, width_share, width_share, block_columns, block_columns, width_share):
        pieces.append(share[:, start : start + extent])
        start += extent

    def unpack(piece):
        rows = piece.reshape(8, -1, blocks * feat).transpose(1, 0, 2).reshape(-1, blocks, feat)
        return rows.transpose(1, 2, 0)[None]

    return (
        final_tokens,
        input_gradient,
        unpack(pieces[4]),
        unpack(pieces[5]),
        pieces[2][None],
        pieces[0][None],
        pieces[1][None],
        pieces[3][None],
        pieces[6][:1],
    )


def solution(mesh):
    body = two_sections if mesh.shape["pipe"] == 2 and mesh.shape["dp"] == 16 else shards
    return jax.shard_map(
        body,
        mesh=mesh,
        in_specs=(
            P(("pipe", "dp"), None),
            P(("pipe", "dp"), None),
            P("pipe", None),
            P("pipe", None, None, None),
            P("pipe", None, None, None),
            P("pipe", None, None),
            P("pipe", None, None),
            P("pipe", None, None),
            P("pipe", None, None),
            P("pipe", None, None, None),
            P("pipe", None),
        ),
        out_specs=(
            P(("pipe", "dp"), None),
            P(("pipe", "dp"), None),
            P("pipe", None, None, "dp"),
            P("pipe", None, None, "dp"),
            P("pipe", None, "dp"),
            P("pipe", None, "dp"),
            P("pipe", None, "dp"),
            P("pipe", None, "dp"),
            P("pipe", "dp"),
        ),
        check_vma=False,
    )
```

```python
import functools
import math

import jax
import jax.numpy as jnp
from jax import lax
from jax.experimental import pallas as pl
from jax.experimental.pallas import tpu as pltpu
from jax.sharding import PartitionSpec as P

precise = lax.Precision.HIGHEST


def from_behind(block, axis, distance):
    devices = range(lax.axis_size(axis))
    route = [(i - distance, i) for i in devices if i - distance in devices]
    return lax.ppermute(block, axis, route)


def gelu_tanh(value):
    return (
        0.5
        * value
        * (1.0 + jnp.tanh(0.7978845608028654 * (value + 0.044715 * value * value * value)))
    )


def selector(indices, group_count):
    groups = jnp.arange(group_count, dtype=jnp.int32)
    return jnp.where(indices[:, None] == groups[None, :], 1.0, 0.0).astype(jnp.float32)


def layer_apply(act, params, pattern, ranks):
    up_blocks, down_blocks, up_left, up_right, down_left, down_right, gain = params
    token_count = act.shape[0]
    feature_width = act.shape[1]
    block_feat = up_blocks.shape[1]
    block_hidden = up_blocks.shape[2]
    group_count = feature_width // block_feat
    hidden_width = up_right.shape[1]
    rank_index = jnp.arange(up_left.shape[0], dtype=jnp.int32)
    up_mask = jnp.where(rank_index < ranks[0], 1.0, 0.0).astype(jnp.float32)
    down_mask = jnp.where(rank_index < ranks[1], 1.0, 0.0).astype(jnp.float32)
    up_source = selector(pattern[0, 0], group_count)
    up_target = selector(pattern[0, 1], group_count)
    down_source = selector(pattern[1, 0], group_count)
    down_target = selector(pattern[1, 1], group_count)
    mean_square = jnp.mean(act * act, axis=1, keepdims=True)
    normed = act * lax.rsqrt(mean_square + 1e-05) * gain
    pieces = jnp.einsum(
        "rgd,kg->rkd",
        normed.reshape(token_count, group_count, block_feat),
        up_source,
        precision=precise,
    )
    up_parts = jnp.einsum("rkd,kdf->rkf", pieces, up_blocks, precision=precise)
    low_coeff = jnp.einsum("rd,qd->rq", normed, up_left, precision=precise) * up_mask
    hidden = jnp.einsum("rq,qf->rf", low_coeff, up_right, precision=precise).reshape(
        token_count, group_count, block_hidden
    )
    hidden = gelu_tanh(hidden + jnp.einsum("rkf,kg->rgf", up_parts, up_target, precision=precise))
    hidden_pieces = jnp.einsum("rgf,kg->rkf", hidden, down_source, precision=precise)
    down_parts = jnp.einsum("rkf,kdf->rkd", hidden_pieces, down_blocks, precision=precise)
    flat_hidden = hidden.reshape(token_count, hidden_width)
    low_down = jnp.einsum("rf,qf->rq", flat_hidden, down_left, precision=precise) * down_mask
    branch = jnp.einsum("rq,qd->rd", low_down, down_right, precision=precise)
    placed = jnp.einsum("rkd,kg->rgd", down_parts, down_target, precision=precise).reshape(
        token_count, feature_width
    )
    return act + branch + placed


def shards(
    tokens,
    cotangent,
    norm_gain,
    up_blocks,
    down_blocks,
    up_left,
    up_right,
    down_left,
    down_right,
    block_pattern,
    rank_used,
):
    sections = lax.axis_size("pipe")
    replicas = lax.axis_size("dp")
    section_index = lax.axis_index("pipe")
    last_section = sections - 1
    micro_rows = tokens.shape[0]
    feature_width = tokens.shape[1]
    section_params = (
        up_blocks[0],
        down_blocks[0],
        up_left[0],
        up_right[0],
        down_left[0],
        down_right[0],
        norm_gain[0],
    )
    section_pattern = block_pattern[0]
    section_ranks = rank_used[0]
    turns = 2 * sections - 1

    def mapped(act, params):
        return layer_apply(act, params, section_pattern, section_ranks)

    def forward_apply(source):
        return mapped(source.astype(jnp.float32), section_params).astype(jnp.bfloat16)

    def forward_spare(source):
        return jnp.zeros_like(source)

    forward_store = tokens
    backward_store = cotangent

    def place_result(handoff_store, emit_rows, result):
        return jnp.where(emit_rows, result, handoff_store)

    def forward_compute(step_index, incoming, handoff_store, saved_inputs):
        micro_index = step_index - section_index
        active = jnp.logical_and(micro_index >= 0, micro_index < sections)
        slot_index = jnp.clip(micro_index, 0, last_section)
        first_rows = handoff_store
        source = jnp.where(section_index == 0, first_rows, incoming)
        result = lax.cond(active, forward_apply, forward_spare, source)
        kept = lax.dynamic_index_in_dim(saved_inputs, slot_index, 0, keepdims=False)
        saved_inputs = lax.dynamic_update_index_in_dim(
            saved_inputs, jnp.where(active, source, kept), slot_index, 0
        )
        emit_rows = jnp.logical_and(active, section_index == last_section)
        handoff_store = place_result(handoff_store, emit_rows, result)
        return (result, handoff_store, saved_inputs)

    def forward_turn(step_index, loop_state):
        incoming, handoff_store, saved_inputs = loop_state
        result, handoff_store, saved_inputs = forward_compute(
            step_index, incoming, handoff_store, saved_inputs
        )
        incoming = from_behind(result, "pipe", 1)
        handoff_store = from_behind(handoff_store, "pipe", -1)
        return (incoming, handoff_store, saved_inputs)

    saved_start = jnp.zeros((sections, micro_rows, feature_width), jnp.bfloat16)
    zero_rows = jnp.zeros((micro_rows, feature_width), jnp.bfloat16)
    loop_state = lax.fori_loop(0, turns - 1, forward_turn, (zero_rows, forward_store, saved_start))
    unused, forward_store, saved_inputs = forward_compute(
        turns - 1, loop_state[0], loop_state[1], loop_state[2]
    )
    zero_grads = tuple((jnp.zeros_like(item) for item in section_params))

    def backward_apply(operands):
        source, upstream, totals = operands
        unused_out, pull = jax.vjp(mapped, source.astype(jnp.float32), section_params)
        act_grad, param_grads = pull(upstream.astype(jnp.float32))
        new_totals = tuple((old + new for old, new in zip(totals, param_grads)))
        return (act_grad.astype(jnp.bfloat16), new_totals)

    def backward_spare(operands):
        return (jnp.zeros_like(operands[0]), operands[2])

    def backward_compute(step_index, incoming, handoff_store, totals):
        micro_index = 2 * last_section - step_index - section_index
        active = jnp.logical_and(micro_index >= 0, micro_index < sections)
        slot_index = jnp.clip(micro_index, 0, last_section)
        top_rows = handoff_store
        upstream = jnp.where(section_index == last_section, top_rows, incoming)
        source = lax.dynamic_index_in_dim(saved_inputs, slot_index, 0, keepdims=False)
        result, totals = lax.cond(
            active, backward_apply, backward_spare, (source, upstream, totals)
        )
        emit_rows = jnp.logical_and(active, section_index == 0)
        handoff_store = place_result(handoff_store, emit_rows, result)
        return (result, handoff_store, totals)

    def backward_turn(step_index, loop_state):
        incoming, handoff_store, totals = loop_state
        result, handoff_store, totals = backward_compute(
            step_index, incoming, handoff_store, totals
        )
        incoming = from_behind(result, "pipe", -1)
        handoff_store = from_behind(handoff_store, "pipe", 1)
        return (incoming, handoff_store, totals)

    loop_state = lax.fori_loop(0, turns - 1, backward_turn, (zero_rows, backward_store, zero_grads))
    unused, backward_store, totals = backward_compute(
        turns - 1, loop_state[0], loop_state[1], loop_state[2]
    )
    expanded = tuple((item[None] for item in totals))
    summed = (
        lax.psum_scatter(expanded[0], "dp", scatter_dimension=3, tiled=True),
        lax.psum_scatter(expanded[1], "dp", scatter_dimension=3, tiled=True),
        lax.psum_scatter(expanded[2], "dp", scatter_dimension=2, tiled=True),
        lax.psum_scatter(expanded[3], "dp", scatter_dimension=2, tiled=True),
        lax.psum_scatter(expanded[4], "dp", scatter_dimension=2, tiled=True),
        lax.psum_scatter(expanded[5], "dp", scatter_dimension=2, tiled=True),
        lax.psum_scatter(expanded[6], "dp", scatter_dimension=1, tiled=True),
    )
    factor = 1.0 / math.sqrt(micro_rows * sections * replicas)
    scaled = [item * factor for item in summed]
    return (
        forward_store,
        backward_store,
        scaled[0],
        scaled[1],
        scaled[2],
        scaled[3],
        scaled[4],
        scaled[5],
        scaled[6],
    )


def masks(ranks, count):
    rank_index = jnp.arange(count, dtype=jnp.int32)
    return (
        jnp.where(rank_index < ranks[0], 1.0, 0.0).astype(jnp.float32),
        jnp.where(rank_index < ranks[1], 1.0, 0.0).astype(jnp.float32),
    )


def parts(x):
    high = x.astype(jnp.bfloat16).astype(jnp.float32)
    return high, x - high


def dot16(a, b, ca, cb):
    return lax.dot_general(
        a.astype(jnp.bfloat16), b.astype(jnp.bfloat16), (((ca,), (cb,)), ((), ())),
        preferred_element_type=jnp.float32,
    )


def expand(a, b):
    ah, al = parts(a)
    bh, bl = parts(b)
    return dot16(jnp.concatenate([ah, al, ah], 1), jnp.concatenate([bh, bh, bl], 0), 1, 0)


def contract(a, b):
    rows, count = a.shape[0], b.shape[0]
    both = dot16(jnp.concatenate(parts(a), 0), jnp.concatenate(parts(b), 0), 1, 1)
    return both[:rows, :count] + both[:rows, count:] + both[rows:, :count]


def outer(a, b):
    ah, al = parts(a)
    bh, bl = parts(b)
    return dot16(jnp.concatenate([ah, al, ah], 0), jnp.concatenate([bh, bh, bl], 0), 0, 0)


def three(a, b, ca, cb):
    ah, al = parts(a)
    bh, bl = parts(b)
    return dot16(ah, bh, ca, cb) + dot16(ah, bl, ca, cb) + dot16(al, bh, ca, cb)


def span(index, width):
    return pl.ds(pl.multiple_of(index * width, 128), width)


def forward_kernel(
    group, pattern, rows, up_wide, down_wide, up_left, up_right, down_left, down_right, gain, masks_ref,
    out, scale_ref, low_ref, pre, low_down_ref, normed_ref, total,
):
    blocks, wide, hid = up_wide.shape
    chunk = pre.shape[1] // 16
    act = rows[...].astype(jnp.float32)
    scale = lax.rsqrt(jnp.mean(act * act, axis=1, keepdims=True) + 1e-05)
    scale_ref[...] = scale
    normed = act * scale * gain[...]
    normed_ref[...] = normed
    low = contract(normed, up_left[...]) * masks_ref[0:1, :]
    low_ref[...] = low

    def fill(i, carry):
        pre[:, span(i, chunk)] = expand(low, up_right[:, span(i, chunk)])
        return carry

    lax.fori_loop(0, 16, fill, 0)
    for k in range(blocks):
        source, target = pattern[k], pattern[blocks + k]
        pre[:, span(target, hid)] += three(normed_ref[:, span(source // group, wide)], up_wide[k], 1, 0)

    def sums(i, carry):
        return carry + contract(gelu_tanh(pre[:, span(i, chunk)]), down_left[:, span(i, chunk)])

    low_down = lax.fori_loop(0, 16, sums, jnp.zeros(low.shape, jnp.float32)) * masks_ref[1:2, :]
    low_down_ref[...] = low_down
    total[...] = act + expand(low_down, down_right[...])
    for k in range(blocks):
        source, target = pattern[2 * blocks + k], pattern[3 * blocks + k]
        part = three(gelu_tanh(pre[:, span(source, hid)]), down_wide[k], 1, 1)
        total[:, span(target // group, wide)] += part
    out[...] = total[...].astype(jnp.bfloat16)


def backward_kernel(
    group, pattern, rows, upstream, scale_ref, low_ref, pre, low_down_ref,
    up_wide, down_wide, up_left, up_right, down_left, down_right, gain, masks_ref,
    act_grad, packed, g_up, g_down, normed_ref, grad_ref, d_pre, d_normed_ref,
):
    blocks, wide, hid = up_wide.shape
    chunk = pre.shape[1] // 16
    narrow = rows.shape[1] // 16
    act = rows[...].astype(jnp.float32)
    scale = scale_ref[...]
    low = low_ref[...]
    low_down = low_down_ref[...]
    normed_ref[...] = act * scale * gain[...]
    grad_ref[...] = upstream[...].astype(jnp.float32)
    d_low_down = contract(grad_ref[...], down_right[...]) * masks_ref[1:2, :]

    def fill(i, carry):
        d_pre[:, span(i, chunk)] = expand(d_low_down, down_left[:, span(i, chunk)])
        return carry

    lax.fori_loop(0, 16, fill, 0)
    for k in range(blocks):
        source, target = pattern[2 * blocks + k], pattern[3 * blocks + k]
        piece = grad_ref[:, span(target // group, wide)]
        d_pre[:, span(source, hid)] += three(piece, down_wide[k], 1, 0)
        g_down[k] = outer(gelu_tanh(pre[:, span(source, hid)]), piece)

    def sums(i, carry):
        here = span(i, chunk)
        value = pre[:, here]
        square = value * value
        tanh = jnp.tanh(0.7978845608028654 * (value + 0.044715 * square * value))
        half = 0.5 * (1.0 + tanh)
        slope = half + 0.5 * value * (1.0 - tanh * tanh) * (
            0.7978845608028654 * (1.0 + 3.0 * 0.044715 * square)
        )
        d_here = d_pre[:, here] * slope
        d_pre[:, here] = d_here
        packed[i, :, 0:chunk] = outer(low, d_here)
        packed[i, :, chunk : 2 * chunk] = outer(d_low_down, value * half)
        return carry + contract(d_here, up_right[:, here])

    d_low = lax.fori_loop(0, 16, sums, jnp.zeros(low.shape, jnp.float32)) * masks_ref[0:1, :]
    d_normed_ref[...] = expand(d_low, up_left[...])
    for k in range(blocks):
        source, target = pattern[k], pattern[blocks + k]
        piece = d_pre[:, span(target, hid)]
        here = span(source // group, wide)
        d_normed_ref[:, here] += three(piece, up_wide[k], 1, 1)
        g_up[k] = outer(piece, normed_ref[:, here])
    d_normed = d_normed_ref[...]
    unit = act * scale
    scaled = d_normed * gain[...]
    grad = grad_ref[...]
    result = grad + scale * (scaled - unit * jnp.mean(scaled * unit, axis=1, keepdims=True))
    act_grad[...] = result.astype(jnp.bfloat16)
    g_gain = jnp.sum(d_normed * unit, axis=0, keepdims=True)
    g_up_left = outer(d_low, normed_ref[...])
    g_down_right = outer(low_down, grad)
    base = 2 * chunk
    for i in range(16):
        cut = slice(i * narrow, (i + 1) * narrow)
        packed[i, :, base : base + narrow] = g_up_left[:, cut]
        packed[i, :, base + narrow : base + 2 * narrow] = g_down_right[:, cut]
        packed[i, :, base + 2 * narrow :] = jnp.broadcast_to(g_gain[:, cut], (8, narrow))


def local_call(body, count, shapes, scratch, cost):
    vmem = pl.BlockSpec(memory_space=pltpu.VMEM)
    return pl.pallas_call(
        body,
        in_specs=[pl.BlockSpec(memory_space=pltpu.SMEM)] + [vmem] * count,
        out_specs=[vmem] * len(shapes),
        out_shape=shapes,
        scratch_shapes=scratch,
        cost_estimate=pl.CostEstimate(flops=cost, bytes_accessed=8000000, transcendentals=800000),
        compiler_params=pltpu.CompilerParams(vmem_limit_bytes=48 * 1024 * 1024),
    )


def widen(blocks, offsets, group):
    chosen = offsets[:, None] % group == jnp.arange(group)[None, :]
    wide = jnp.where(chosen[:, :, None, None], blocks[:, None], 0.0)
    return wide.reshape(blocks.shape[0], group * blocks.shape[1], blocks.shape[2])


def prepare(params, pattern, ranks):
    up_blocks, down_blocks, up_left, up_right, down_left, down_right, gain = params
    group = 4
    return (
        widen(up_blocks, pattern[0, 0], group),
        widen(down_blocks, pattern[1, 1], group),
        up_left,
        up_right,
        down_left,
        down_right,
        gain[None],
        jnp.stack(masks(ranks, up_left.shape[0])),
    )


def forward_pass(rows, ready, pattern):
    count, width = rows.shape
    rank, hidden = ready[3].shape
    f32 = jnp.float32
    shape = jax.ShapeDtypeStruct
    out, scale, low, pre, low_down = local_call(
        functools.partial(forward_kernel, 4),
        9,
        [
            shape((count, width), jnp.bfloat16),
            shape((count, 1), f32),
            shape((count, rank), f32),
            shape((count, hidden), f32),
            shape((count, rank), f32),
        ],
        [pltpu.VMEM((count, width), f32), pltpu.VMEM((count, width), f32)],
        100000000,
    )(pattern.reshape(-1), rows, *ready)
    return out, (scale, low, pre, low_down)


def backward_pass(rows, upstream, saved, ready, pattern, replicas):
    count, width = rows.shape
    rank, hidden = ready[3].shape
    blocks, wide, hid = ready[0].shape
    f32 = jnp.float32
    shape = jax.ShapeDtypeStruct
    act_grad, packed, g_up, g_down = local_call(
        functools.partial(backward_kernel, 4),
        14,
        [
            shape((count, width), jnp.bfloat16),
            shape((16, rank, (2 * hidden + 3 * width) // 16), f32),
            shape((blocks, hid, wide), f32),
            shape((blocks, hid, wide), f32),
        ],
        [
            pltpu.VMEM((count, width), f32),
            pltpu.VMEM((count, width), f32),
            pltpu.VMEM((count, hidden), f32),
            pltpu.VMEM((count, width), f32),
        ],
        200000000,
    )(pattern.reshape(-1), rows, upstream, *saved, *ready)

    def block_share(g, offsets):
        chosen = offsets[:, None] % 4 == jnp.arange(4)[None, :]
        cut = jnp.sum(jnp.where(chosen[:, None, :, None], g.reshape(blocks, hid, 4, -1), 0.0), axis=2)
        whole = cut.transpose(1, 0, 2).reshape(hid, -1)
        eighths = whole.reshape(replicas, -1, 8, whole.shape[1]).transpose(0, 2, 1, 3)
        return eighths.reshape(replicas, 8, -1)

    return act_grad, jnp.concatenate(
        [packed, block_share(g_up, pattern[0, 0]), block_share(g_down, pattern[1, 1])], axis=2
    )


def reduce_shares(packed):
    return lax.psum_scatter(packed, "dp", scatter_dimension=0, tiled=False)


def two_sections(
    tokens,
    cotangent,
    norm_gain,
    up_blocks,
    down_blocks,
    up_left,
    up_right,
    down_left,
    down_right,
    block_pattern,
    rank_used,
):
    replicas = lax.axis_size("dp")
    section = lax.axis_index("pipe")
    count, width = tokens.shape
    params = (
        up_blocks[0],
        down_blocks[0],
        up_left[0],
        up_right[0],
        down_left[0],
        down_right[0],
        norm_gain[0],
    )
    pattern = block_pattern[0]
    ranks = rank_used[0]
    ready = prepare(params, pattern, ranks)
    forth, back = [(0, 1)], [(1, 0)]
    first = jnp.concatenate([tokens, lax.ppermute(tokens, "pipe", back)], axis=0)
    top = jnp.concatenate([lax.ppermute(cotangent, "pipe", forth), cotangent], axis=0)

    def run(rows):
        return forward_pass(rows, ready, pattern)

    def skip_forward(rows):
        return jax.tree.map(lambda t: jnp.zeros(t.shape, t.dtype), jax.eval_shape(run, rows))

    result, saved = lax.cond(section == 0, run, skip_forward, first)
    second = lax.ppermute(result, "pipe", forth)

    def last(operands):
        rows, upstream = operands
        out, kept = run(rows)
        below, packed = backward_pass(rows, upstream, kept, ready, pattern, replicas)
        return out, below, packed

    def skip_last(operands):
        return jax.tree.map(lambda t: jnp.zeros(t.shape, t.dtype), jax.eval_shape(last, operands))

    final, below, packed = lax.cond(section == 1, last, skip_last, (second, top))
    from_above = lax.ppermute(below, "pipe", back)
    final_early = lax.ppermute(final[:count], "pipe", back)

    def first_back(operands):
        upstream, kept, unused = operands
        return backward_pass(first, upstream, kept, ready, pattern, replicas)

    def skip_back(operands):
        return operands[0], operands[2]

    bottom, packed = lax.cond(section == 0, first_back, skip_back, (from_above, saved, packed))
    bottom_late = lax.ppermute(bottom[count:], "pipe", forth)
    final_tokens = jnp.where(section == 0, final_early, final[count:])
    input_gradient = jnp.where(section == 0, bottom[:count], bottom_late)
    factor = 1.0 / math.sqrt(count * 2 * replicas)
    share = reduce_shares(packed) * factor
    blocks, feat, hid = params[0].shape
    hidden_share = params[3].shape[1] // replicas
    width_share = width // replicas
    block_columns = hid // replicas // 8 * blocks * feat
    pieces = []
    start = 0
    for extent in (hidden_share, hidden_share, width_share, width_share, width_share, block_columns, block_columns):
        pieces.append(share[:, start : start + extent])
        start += extent

    def unpack(piece):
        rows = piece.reshape(8, -1, blocks * feat).transpose(1, 0, 2).reshape(-1, blocks, feat)
        return rows.transpose(1, 2, 0)[None]

    return (
        final_tokens,
        input_gradient,
        unpack(pieces[5]),
        unpack(pieces[6]),
        pieces[2][None],
        pieces[0][None],
        pieces[1][None],
        pieces[3][None],
        pieces[4][:1],
    )


def solution(mesh):
    body = two_sections if mesh.shape["pipe"] == 2 and mesh.shape["dp"] == 16 else shards
    return jax.shard_map(
        body,
        mesh=mesh,
        in_specs=(
            P(("pipe", "dp"), None),
            P(("pipe", "dp"), None),
            P("pipe", None),
            P("pipe", None, None, None),
            P("pipe", None, None, None),
            P("pipe", None, None),
            P("pipe", None, None),
            P("pipe", None, None),
            P("pipe", None, None),
            P("pipe", None, None, None),
            P("pipe", None),
        ),
        out_specs=(
            P(("pipe", "dp"), None),
            P(("pipe", "dp"), None),
            P("pipe", None, None, "dp"),
            P("pipe", None, None, "dp"),
            P("pipe", None, "dp"),
            P("pipe", None, "dp"),
            P("pipe", None, "dp"),
            P("pipe", None, "dp"),
            P("pipe", "dp"),
        ),
        check_vma=False,
    )
```

```python
import functools
import math

import jax
import jax.numpy as jnp
from jax import lax
from jax.experimental import pallas as pl
from jax.experimental.pallas import tpu as pltpu
from jax.sharding import PartitionSpec as P

precise = lax.Precision.HIGHEST


def from_behind(block, axis, distance):
    devices = range(lax.axis_size(axis))
    route = [(i - distance, i) for i in devices if i - distance in devices]
    return lax.ppermute(block, axis, route)


def gelu_tanh(value):
    return (
        0.5
        * value
        * (1.0 + jnp.tanh(0.7978845608028654 * (value + 0.044715 * value * value * value)))
    )


def selector(indices, group_count):
    groups = jnp.arange(group_count, dtype=jnp.int32)
    return jnp.where(indices[:, None] == groups[None, :], 1.0, 0.0).astype(jnp.float32)


def layer_apply(act, params, pattern, ranks):
    up_blocks, down_blocks, up_left, up_right, down_left, down_right, gain = params
    token_count = act.shape[0]
    feature_width = act.shape[1]
    block_feat = up_blocks.shape[1]
    block_hidden = up_blocks.shape[2]
    group_count = feature_width // block_feat
    hidden_width = up_right.shape[1]
    rank_index = jnp.arange(up_left.shape[0], dtype=jnp.int32)
    up_mask = jnp.where(rank_index < ranks[0], 1.0, 0.0).astype(jnp.float32)
    down_mask = jnp.where(rank_index < ranks[1], 1.0, 0.0).astype(jnp.float32)
    up_source = selector(pattern[0, 0], group_count)
    up_target = selector(pattern[0, 1], group_count)
    down_source = selector(pattern[1, 0], group_count)
    down_target = selector(pattern[1, 1], group_count)
    mean_square = jnp.mean(act * act, axis=1, keepdims=True)
    normed = act * lax.rsqrt(mean_square + 1e-05) * gain
    pieces = jnp.einsum(
        "rgd,kg->rkd",
        normed.reshape(token_count, group_count, block_feat),
        up_source,
        precision=precise,
    )
    up_parts = jnp.einsum("rkd,kdf->rkf", pieces, up_blocks, precision=precise)
    low_coeff = jnp.einsum("rd,qd->rq", normed, up_left, precision=precise) * up_mask
    hidden = jnp.einsum("rq,qf->rf", low_coeff, up_right, precision=precise).reshape(
        token_count, group_count, block_hidden
    )
    hidden = gelu_tanh(hidden + jnp.einsum("rkf,kg->rgf", up_parts, up_target, precision=precise))
    hidden_pieces = jnp.einsum("rgf,kg->rkf", hidden, down_source, precision=precise)
    down_parts = jnp.einsum("rkf,kdf->rkd", hidden_pieces, down_blocks, precision=precise)
    flat_hidden = hidden.reshape(token_count, hidden_width)
    low_down = jnp.einsum("rf,qf->rq", flat_hidden, down_left, precision=precise) * down_mask
    branch = jnp.einsum("rq,qd->rd", low_down, down_right, precision=precise)
    placed = jnp.einsum("rkd,kg->rgd", down_parts, down_target, precision=precise).reshape(
        token_count, feature_width
    )
    return act + branch + placed


def shards(
    tokens,
    cotangent,
    norm_gain,
    up_blocks,
    down_blocks,
    up_left,
    up_right,
    down_left,
    down_right,
    block_pattern,
    rank_used,
):
    sections = lax.axis_size("pipe")
    replicas = lax.axis_size("dp")
    section_index = lax.axis_index("pipe")
    last_section = sections - 1
    micro_rows = tokens.shape[0]
    feature_width = tokens.shape[1]
    section_params = (
        up_blocks[0],
        down_blocks[0],
        up_left[0],
        up_right[0],
        down_left[0],
        down_right[0],
        norm_gain[0],
    )
    section_pattern = block_pattern[0]
    section_ranks = rank_used[0]
    turns = 2 * sections - 1

    def mapped(act, params):
        return layer_apply(act, params, section_pattern, section_ranks)

    def forward_apply(source):
        return mapped(source.astype(jnp.float32), section_params).astype(jnp.bfloat16)

    def forward_spare(source):
        return jnp.zeros_like(source)

    forward_store = tokens
    backward_store = cotangent

    def place_result(handoff_store, emit_rows, result):
        return jnp.where(emit_rows, result, handoff_store)

    def forward_compute(step_index, incoming, handoff_store, saved_inputs):
        micro_index = step_index - section_index
        active = jnp.logical_and(micro_index >= 0, micro_index < sections)
        slot_index = jnp.clip(micro_index, 0, last_section)
        first_rows = handoff_store
        source = jnp.where(section_index == 0, first_rows, incoming)
        result = lax.cond(active, forward_apply, forward_spare, source)
        kept = lax.dynamic_index_in_dim(saved_inputs, slot_index, 0, keepdims=False)
        saved_inputs = lax.dynamic_update_index_in_dim(
            saved_inputs, jnp.where(active, source, kept), slot_index, 0
        )
        emit_rows = jnp.logical_and(active, section_index == last_section)
        handoff_store = place_result(handoff_store, emit_rows, result)
        return (result, handoff_store, saved_inputs)

    def forward_turn(step_index, loop_state):
        incoming, handoff_store, saved_inputs = loop_state
        result, handoff_store, saved_inputs = forward_compute(
            step_index, incoming, handoff_store, saved_inputs
        )
        incoming = from_behind(result, "pipe", 1)
        handoff_store = from_behind(handoff_store, "pipe", -1)
        return (incoming, handoff_store, saved_inputs)

    saved_start = jnp.zeros((sections, micro_rows, feature_width), jnp.bfloat16)
    zero_rows = jnp.zeros((micro_rows, feature_width), jnp.bfloat16)
    loop_state = lax.fori_loop(0, turns - 1, forward_turn, (zero_rows, forward_store, saved_start))
    unused, forward_store, saved_inputs = forward_compute(
        turns - 1, loop_state[0], loop_state[1], loop_state[2]
    )
    zero_grads = tuple((jnp.zeros_like(item) for item in section_params))

    def backward_apply(operands):
        source, upstream, totals = operands
        unused_out, pull = jax.vjp(mapped, source.astype(jnp.float32), section_params)
        act_grad, param_grads = pull(upstream.astype(jnp.float32))
        new_totals = tuple((old + new for old, new in zip(totals, param_grads)))
        return (act_grad.astype(jnp.bfloat16), new_totals)

    def backward_spare(operands):
        return (jnp.zeros_like(operands[0]), operands[2])

    def backward_compute(step_index, incoming, handoff_store, totals):
        micro_index = 2 * last_section - step_index - section_index
        active = jnp.logical_and(micro_index >= 0, micro_index < sections)
        slot_index = jnp.clip(micro_index, 0, last_section)
        top_rows = handoff_store
        upstream = jnp.where(section_index == last_section, top_rows, incoming)
        source = lax.dynamic_index_in_dim(saved_inputs, slot_index, 0, keepdims=False)
        result, totals = lax.cond(
            active, backward_apply, backward_spare, (source, upstream, totals)
        )
        emit_rows = jnp.logical_and(active, section_index == 0)
        handoff_store = place_result(handoff_store, emit_rows, result)
        return (result, handoff_store, totals)

    def backward_turn(step_index, loop_state):
        incoming, handoff_store, totals = loop_state
        result, handoff_store, totals = backward_compute(
            step_index, incoming, handoff_store, totals
        )
        incoming = from_behind(result, "pipe", -1)
        handoff_store = from_behind(handoff_store, "pipe", 1)
        return (incoming, handoff_store, totals)

    loop_state = lax.fori_loop(0, turns - 1, backward_turn, (zero_rows, backward_store, zero_grads))
    unused, backward_store, totals = backward_compute(
        turns - 1, loop_state[0], loop_state[1], loop_state[2]
    )
    expanded = tuple((item[None] for item in totals))
    summed = (
        lax.psum_scatter(expanded[0], "dp", scatter_dimension=3, tiled=True),
        lax.psum_scatter(expanded[1], "dp", scatter_dimension=3, tiled=True),
        lax.psum_scatter(expanded[2], "dp", scatter_dimension=2, tiled=True),
        lax.psum_scatter(expanded[3], "dp", scatter_dimension=2, tiled=True),
        lax.psum_scatter(expanded[4], "dp", scatter_dimension=2, tiled=True),
        lax.psum_scatter(expanded[5], "dp", scatter_dimension=2, tiled=True),
        lax.psum_scatter(expanded[6], "dp", scatter_dimension=1, tiled=True),
    )
    factor = 1.0 / math.sqrt(micro_rows * sections * replicas)
    scaled = [item * factor for item in summed]
    return (
        forward_store,
        backward_store,
        scaled[0],
        scaled[1],
        scaled[2],
        scaled[3],
        scaled[4],
        scaled[5],
        scaled[6],
    )


def masks(ranks, count):
    rank_index = jnp.arange(count, dtype=jnp.int32)
    return (
        jnp.where(rank_index < ranks[0], 1.0, 0.0).astype(jnp.float32),
        jnp.where(rank_index < ranks[1], 1.0, 0.0).astype(jnp.float32),
    )


def parts(x):
    high = x.astype(jnp.bfloat16).astype(jnp.float32)
    return high, x - high


def dot16(a, b, ca, cb):
    return lax.dot_general(
        a.astype(jnp.bfloat16), b.astype(jnp.bfloat16), (((ca,), (cb,)), ((), ())),
        preferred_element_type=jnp.float32,
    )


def expand(a, b):
    ah, al = parts(a)
    bh, bl = parts(b)
    return dot16(jnp.concatenate([ah, al, ah], 1), jnp.concatenate([bh, bh, bl], 0), 1, 0)


def contract(a, b):
    rows, count = a.shape[0], b.shape[0]
    both = dot16(jnp.concatenate(parts(a), 0), jnp.concatenate(parts(b), 0), 1, 1)
    return both[:rows, :count] + both[:rows, count:] + both[rows:, :count]


def outer(a, b):
    ah, al = parts(a)
    bh, bl = parts(b)
    return dot16(jnp.concatenate([ah, al, ah], 0), jnp.concatenate([bh, bh, bl], 0), 0, 0)


def three(a, b, ca, cb):
    ah, al = parts(a)
    bh, bl = parts(b)
    return dot16(ah, bh, ca, cb) + dot16(ah, bl, ca, cb) + dot16(al, bh, ca, cb)


def span(index, width):
    return pl.ds(pl.multiple_of(index * width, 128), width)


def forward_kernel(
    group, pattern, rows, up_wide, down_wide, up_left, up_right, down_left, down_right, gain, masks_ref,
    out, scale_ref, low_ref, pre, low_down_ref, normed_ref, total,
):
    blocks, wide, hid = up_wide.shape
    chunk = pre.shape[1] // 16
    act = rows[...].astype(jnp.float32)
    scale = lax.rsqrt(jnp.mean(act * act, axis=1, keepdims=True) + 1e-05)
    scale_ref[...] = scale
    normed = act * scale * gain[...]
    normed_ref[...] = normed
    low = contract(normed, up_left[...]) * masks_ref[0:1, :]
    low_ref[...] = low

    def fill(i, carry):
        pre[:, span(i, chunk)] = expand(low, up_right[:, span(i, chunk)])
        return carry

    lax.fori_loop(0, 16, fill, 0)
    for k in range(blocks):
        source, target = pattern[k], pattern[blocks + k]
        pre[:, span(target, hid)] += three(normed_ref[:, span(source // group, wide)], up_wide[k], 1, 0)

    def sums(i, carry):
        return carry + contract(gelu_tanh(pre[:, span(i, chunk)]), down_left[:, span(i, chunk)])

    low_down = lax.fori_loop(0, 16, sums, jnp.zeros(low.shape, jnp.float32)) * masks_ref[1:2, :]
    low_down_ref[...] = low_down
    total[...] = act + expand(low_down, down_right[...])
    for k in range(blocks):
        source, target = pattern[2 * blocks + k], pattern[3 * blocks + k]
        part = three(gelu_tanh(pre[:, span(source, hid)]), down_wide[k], 1, 1)
        total[:, span(target // group, wide)] += part
    out[...] = total[...].astype(jnp.bfloat16)


def backward_kernel(
    group, pattern, rows, upstream, scale_ref, low_ref, pre, low_down_ref,
    up_wide, down_wide, up_left, up_right, down_left, down_right, gain, masks_ref,
    act_grad, packed, g_up, g_down, normed_ref, grad_ref, d_pre, d_normed_ref,
):
    blocks, wide, hid = up_wide.shape
    chunk = pre.shape[1] // 16
    narrow = rows.shape[1] // 16
    act = rows[...].astype(jnp.float32)
    scale = scale_ref[...]
    low = low_ref[...]
    low_down = low_down_ref[...]
    normed_ref[...] = act * scale * gain[...]
    grad_ref[...] = upstream[...].astype(jnp.float32)
    d_low_down = contract(grad_ref[...], down_right[...]) * masks_ref[1:2, :]

    def fill(i, carry):
        d_pre[:, span(i, chunk)] = expand(d_low_down, down_left[:, span(i, chunk)])
        return carry

    lax.fori_loop(0, 16, fill, 0)
    for k in range(blocks):
        source, target = pattern[2 * blocks + k], pattern[3 * blocks + k]
        piece = grad_ref[:, span(target // group, wide)]
        d_pre[:, span(source, hid)] += three(piece, down_wide[k], 1, 0)
        g_down[k] = outer(gelu_tanh(pre[:, span(source, hid)]), piece)

    def sums(i, carry):
        here = span(i, chunk)
        value = pre[:, here]
        square = value * value
        tanh = jnp.tanh(0.7978845608028654 * (value + 0.044715 * square * value))
        half = 0.5 * (1.0 + tanh)
        slope = half + 0.5 * value * (1.0 - tanh * tanh) * (
            0.7978845608028654 * (1.0 + 3.0 * 0.044715 * square)
        )
        d_here = d_pre[:, here] * slope
        d_pre[:, here] = d_here
        packed[i, :, 0:chunk] = outer(low, d_here)
        packed[i, :, chunk : 2 * chunk] = outer(d_low_down, value * half)
        return carry + contract(d_here, up_right[:, here])

    d_low = lax.fori_loop(0, 16, sums, jnp.zeros(low.shape, jnp.float32)) * masks_ref[0:1, :]
    d_normed_ref[...] = expand(d_low, up_left[...])
    for k in range(blocks):
        source, target = pattern[k], pattern[blocks + k]
        piece = d_pre[:, span(target, hid)]
        here = span(source // group, wide)
        d_normed_ref[:, here] += three(piece, up_wide[k], 1, 1)
        g_up[k] = outer(piece, normed_ref[:, here])
    d_normed = d_normed_ref[...]
    unit = act * scale
    scaled = d_normed * gain[...]
    grad = grad_ref[...]
    result = grad + scale * (scaled - unit * jnp.mean(scaled * unit, axis=1, keepdims=True))
    act_grad[...] = result.astype(jnp.bfloat16)
    g_gain = jnp.sum(d_normed * unit, axis=0, keepdims=True)
    g_up_left = outer(d_low, normed_ref[...])
    g_down_right = outer(low_down, grad)
    base = 2 * chunk
    for i in range(16):
        cut = slice(i * narrow, (i + 1) * narrow)
        packed[i, :, base : base + narrow] = g_up_left[:, cut]
        packed[i, :, base + narrow : base + 2 * narrow] = g_down_right[:, cut]
        packed[i, :, base + 2 * narrow :] = jnp.broadcast_to(g_gain[:, cut], (8, narrow))


def local_call(body, count, shapes, scratch, cost):
    vmem = pl.BlockSpec(memory_space=pltpu.VMEM)
    return pl.pallas_call(
        body,
        in_specs=[pl.BlockSpec(memory_space=pltpu.SMEM)] + [vmem] * count,
        out_specs=[vmem] * len(shapes),
        out_shape=shapes,
        scratch_shapes=scratch,
        cost_estimate=pl.CostEstimate(flops=cost, bytes_accessed=8000000, transcendentals=800000),
        compiler_params=pltpu.CompilerParams(vmem_limit_bytes=48 * 1024 * 1024),
    )


def widen(blocks, offsets, group):
    chosen = offsets[:, None] % group == jnp.arange(group)[None, :]
    wide = jnp.where(chosen[:, :, None, None], blocks[:, None], 0.0)
    return wide.reshape(blocks.shape[0], group * blocks.shape[1], blocks.shape[2])


def prepare(params, pattern, ranks):
    up_blocks, down_blocks, up_left, up_right, down_left, down_right, gain = params
    group = 4
    return (
        widen(up_blocks, pattern[0, 0], group),
        widen(down_blocks, pattern[1, 1], group),
        up_left,
        up_right,
        down_left,
        down_right,
        gain[None],
        jnp.stack(masks(ranks, up_left.shape[0])),
    )


def forward_pass(rows, ready, pattern):
    count, width = rows.shape
    rank, hidden = ready[3].shape
    f32 = jnp.float32
    shape = jax.ShapeDtypeStruct
    out, scale, low, pre, low_down = local_call(
        functools.partial(forward_kernel, 4),
        9,
        [
            shape((count, width), jnp.bfloat16),
            shape((count, 1), f32),
            shape((count, rank), f32),
            shape((count, hidden), f32),
            shape((count, rank), f32),
        ],
        [pltpu.VMEM((count, width), f32), pltpu.VMEM((count, width), f32)],
        100000000,
    )(pattern.reshape(-1), rows, *ready)
    return out, (scale, low, pre, low_down)


def backward_pass(rows, upstream, saved, ready, pattern):
    count, width = rows.shape
    rank, hidden = ready[3].shape
    blocks, wide, hid = ready[0].shape
    f32 = jnp.float32
    shape = jax.ShapeDtypeStruct
    act_grad, packed, g_up, g_down = local_call(
        functools.partial(backward_kernel, 4),
        14,
        [
            shape((count, width), jnp.bfloat16),
            shape((16, rank, (2 * hidden + 3 * width) // 16), f32),
            shape((blocks, hid, wide), f32),
            shape((blocks, hid, wide), f32),
        ],
        [
            pltpu.VMEM((count, width), f32),
            pltpu.VMEM((count, width), f32),
            pltpu.VMEM((count, hidden), f32),
            pltpu.VMEM((count, width), f32),
        ],
        200000000,
    )(pattern.reshape(-1), rows, upstream, *saved, *ready)

    return act_grad, (packed, g_up, g_down)


def pack(grads, pattern, replicas):
    packed, g_up, g_down = grads
    blocks, hid = g_up.shape[:2]

    def block_share(g, offsets):
        chosen = offsets[:, None] % 4 == jnp.arange(4)[None, :]
        cut = jnp.sum(jnp.where(chosen[:, None, :, None], g.reshape(blocks, hid, 4, -1), 0.0), axis=2)
        whole = cut.transpose(1, 0, 2).reshape(hid, -1)
        eighths = whole.reshape(replicas, -1, 8, whole.shape[1]).transpose(0, 2, 1, 3)
        return eighths.reshape(replicas, 8, -1)

    return jnp.concatenate(
        [packed, block_share(g_up, pattern[0, 0]), block_share(g_down, pattern[1, 1])], axis=2
    )


def reduce_shares(packed):
    return lax.psum_scatter(packed, "dp", scatter_dimension=0, tiled=False)


def two_sections(
    tokens,
    cotangent,
    norm_gain,
    up_blocks,
    down_blocks,
    up_left,
    up_right,
    down_left,
    down_right,
    block_pattern,
    rank_used,
):
    replicas = lax.axis_size("dp")
    section = lax.axis_index("pipe")
    count, width = tokens.shape
    params = (
        up_blocks[0],
        down_blocks[0],
        up_left[0],
        up_right[0],
        down_left[0],
        down_right[0],
        norm_gain[0],
    )
    pattern = block_pattern[0]
    ranks = rank_used[0]
    ready = prepare(params, pattern, ranks)
    forth, back = [(0, 1)], [(1, 0)]
    first = jnp.concatenate([tokens, lax.ppermute(tokens, "pipe", back)], axis=0)
    top = jnp.concatenate([lax.ppermute(cotangent, "pipe", forth), cotangent], axis=0)

    def run(rows):
        return forward_pass(rows, ready, pattern)

    def skip_forward(rows):
        return jax.tree.map(lambda t: jnp.zeros(t.shape, t.dtype), jax.eval_shape(run, rows))

    result, saved = lax.cond(section == 0, run, skip_forward, first)
    second = lax.ppermute(result, "pipe", forth)

    def last(operands):
        rows, upstream = operands
        out, kept = run(rows)
        below, packed = backward_pass(rows, upstream, kept, ready, pattern)
        return out, below, packed

    def skip_last(operands):
        return jax.tree.map(lambda t: jnp.zeros(t.shape, t.dtype), jax.eval_shape(last, operands))

    final, below, packed = lax.cond(section == 1, last, skip_last, (second, top))
    from_above = lax.ppermute(below, "pipe", back)
    final_early = lax.ppermute(final[:count], "pipe", back)

    def first_back(operands):
        upstream, kept, unused = operands
        return backward_pass(first, upstream, kept, ready, pattern)

    def skip_back(operands):
        return operands[0], operands[2]

    bottom, packed = lax.cond(section == 0, first_back, skip_back, (from_above, saved, packed))
    bottom_late = lax.ppermute(bottom[count:], "pipe", forth)
    final_tokens = jnp.where(section == 0, final_early, final[count:])
    input_gradient = jnp.where(section == 0, bottom[:count], bottom_late)
    factor = 1.0 / math.sqrt(count * 2 * replicas)
    share = reduce_shares(pack(packed, pattern, replicas)) * factor
    blocks, feat, hid = params[0].shape
    hidden_share = params[3].shape[1] // replicas
    width_share = width // replicas
    block_columns = hid // replicas // 8 * blocks * feat
    pieces = []
    start = 0
    for extent in (hidden_share, hidden_share, width_share, width_share, width_share, block_columns, block_columns):
        pieces.append(share[:, start : start + extent])
        start += extent

    def unpack(piece):
        rows = piece.reshape(8, -1, blocks * feat).transpose(1, 0, 2).reshape(-1, blocks, feat)
        return rows.transpose(1, 2, 0)[None]

    return (
        final_tokens,
        input_gradient,
        unpack(pieces[5]),
        unpack(pieces[6]),
        pieces[2][None],
        pieces[0][None],
        pieces[1][None],
        pieces[3][None],
        pieces[4][:1],
    )


def solution(mesh):
    body = two_sections if mesh.shape["pipe"] == 2 and mesh.shape["dp"] == 16 else shards
    return jax.shard_map(
        body,
        mesh=mesh,
        in_specs=(
            P(("pipe", "dp"), None),
            P(("pipe", "dp"), None),
            P("pipe", None),
            P("pipe", None, None, None),
            P("pipe", None, None, None),
            P("pipe", None, None),
            P("pipe", None, None),
            P("pipe", None, None),
            P("pipe", None, None),
            P("pipe", None, None, None),
            P("pipe", None),
        ),
        out_specs=(
            P(("pipe", "dp"), None),
            P(("pipe", "dp"), None),
            P("pipe", None, None, "dp"),
            P("pipe", None, None, "dp"),
            P("pipe", None, "dp"),
            P("pipe", None, "dp"),
            P("pipe", None, "dp"),
            P("pipe", None, "dp"),
            P("pipe", "dp"),
        ),
        check_vma=False,
    )
```

```python
import functools
import math

import jax
import jax.numpy as jnp
from jax import lax
from jax.experimental import pallas as pl
from jax.experimental.pallas import tpu as pltpu
from jax.sharding import PartitionSpec as P

precise = lax.Precision.HIGHEST


def from_behind(block, axis, distance):
    devices = range(lax.axis_size(axis))
    route = [(i - distance, i) for i in devices if i - distance in devices]
    return lax.ppermute(block, axis, route)


def gelu_tanh(value):
    return (
        0.5
        * value
        * (1.0 + jnp.tanh(0.7978845608028654 * (value + 0.044715 * value * value * value)))
    )


def selector(indices, group_count):
    groups = jnp.arange(group_count, dtype=jnp.int32)
    return jnp.where(indices[:, None] == groups[None, :], 1.0, 0.0).astype(jnp.float32)


def layer_apply(act, params, pattern, ranks):
    up_blocks, down_blocks, up_left, up_right, down_left, down_right, gain = params
    token_count = act.shape[0]
    feature_width = act.shape[1]
    block_feat = up_blocks.shape[1]
    block_hidden = up_blocks.shape[2]
    group_count = feature_width // block_feat
    hidden_width = up_right.shape[1]
    rank_index = jnp.arange(up_left.shape[0], dtype=jnp.int32)
    up_mask = jnp.where(rank_index < ranks[0], 1.0, 0.0).astype(jnp.float32)
    down_mask = jnp.where(rank_index < ranks[1], 1.0, 0.0).astype(jnp.float32)
    up_source = selector(pattern[0, 0], group_count)
    up_target = selector(pattern[0, 1], group_count)
    down_source = selector(pattern[1, 0], group_count)
    down_target = selector(pattern[1, 1], group_count)
    mean_square = jnp.mean(act * act, axis=1, keepdims=True)
    normed = act * lax.rsqrt(mean_square + 1e-05) * gain
    pieces = jnp.einsum(
        "rgd,kg->rkd",
        normed.reshape(token_count, group_count, block_feat),
        up_source,
        precision=precise,
    )
    up_parts = jnp.einsum("rkd,kdf->rkf", pieces, up_blocks, precision=precise)
    low_coeff = jnp.einsum("rd,qd->rq", normed, up_left, precision=precise) * up_mask
    hidden = jnp.einsum("rq,qf->rf", low_coeff, up_right, precision=precise).reshape(
        token_count, group_count, block_hidden
    )
    hidden = gelu_tanh(hidden + jnp.einsum("rkf,kg->rgf", up_parts, up_target, precision=precise))
    hidden_pieces = jnp.einsum("rgf,kg->rkf", hidden, down_source, precision=precise)
    down_parts = jnp.einsum("rkf,kdf->rkd", hidden_pieces, down_blocks, precision=precise)
    flat_hidden = hidden.reshape(token_count, hidden_width)
    low_down = jnp.einsum("rf,qf->rq", flat_hidden, down_left, precision=precise) * down_mask
    branch = jnp.einsum("rq,qd->rd", low_down, down_right, precision=precise)
    placed = jnp.einsum("rkd,kg->rgd", down_parts, down_target, precision=precise).reshape(
        token_count, feature_width
    )
    return act + branch + placed


def shards(
    tokens,
    cotangent,
    norm_gain,
    up_blocks,
    down_blocks,
    up_left,
    up_right,
    down_left,
    down_right,
    block_pattern,
    rank_used,
):
    sections = lax.axis_size("pipe")
    replicas = lax.axis_size("dp")
    section_index = lax.axis_index("pipe")
    last_section = sections - 1
    micro_rows = tokens.shape[0]
    feature_width = tokens.shape[1]
    section_params = (
        up_blocks[0],
        down_blocks[0],
        up_left[0],
        up_right[0],
        down_left[0],
        down_right[0],
        norm_gain[0],
    )
    section_pattern = block_pattern[0]
    section_ranks = rank_used[0]
    turns = 2 * sections - 1

    def mapped(act, params):
        return layer_apply(act, params, section_pattern, section_ranks)

    def forward_apply(source):
        return mapped(source.astype(jnp.float32), section_params).astype(jnp.bfloat16)

    def forward_spare(source):
        return jnp.zeros_like(source)

    forward_store = tokens
    backward_store = cotangent

    def place_result(handoff_store, emit_rows, result):
        return jnp.where(emit_rows, result, handoff_store)

    def forward_compute(step_index, incoming, handoff_store, saved_inputs):
        micro_index = step_index - section_index
        active = jnp.logical_and(micro_index >= 0, micro_index < sections)
        slot_index = jnp.clip(micro_index, 0, last_section)
        first_rows = handoff_store
        source = jnp.where(section_index == 0, first_rows, incoming)
        result = lax.cond(active, forward_apply, forward_spare, source)
        kept = lax.dynamic_index_in_dim(saved_inputs, slot_index, 0, keepdims=False)
        saved_inputs = lax.dynamic_update_index_in_dim(
            saved_inputs, jnp.where(active, source, kept), slot_index, 0
        )
        emit_rows = jnp.logical_and(active, section_index == last_section)
        handoff_store = place_result(handoff_store, emit_rows, result)
        return (result, handoff_store, saved_inputs)

    def forward_turn(step_index, loop_state):
        incoming, handoff_store, saved_inputs = loop_state
        result, handoff_store, saved_inputs = forward_compute(
            step_index, incoming, handoff_store, saved_inputs
        )
        incoming = from_behind(result, "pipe", 1)
        handoff_store = from_behind(handoff_store, "pipe", -1)
        return (incoming, handoff_store, saved_inputs)

    saved_start = jnp.zeros((sections, micro_rows, feature_width), jnp.bfloat16)
    zero_rows = jnp.zeros((micro_rows, feature_width), jnp.bfloat16)
    loop_state = lax.fori_loop(0, turns - 1, forward_turn, (zero_rows, forward_store, saved_start))
    unused, forward_store, saved_inputs = forward_compute(
        turns - 1, loop_state[0], loop_state[1], loop_state[2]
    )
    zero_grads = tuple((jnp.zeros_like(item) for item in section_params))

    def backward_apply(operands):
        source, upstream, totals = operands
        unused_out, pull = jax.vjp(mapped, source.astype(jnp.float32), section_params)
        act_grad, param_grads = pull(upstream.astype(jnp.float32))
        new_totals = tuple((old + new for old, new in zip(totals, param_grads)))
        return (act_grad.astype(jnp.bfloat16), new_totals)

    def backward_spare(operands):
        return (jnp.zeros_like(operands[0]), operands[2])

    def backward_compute(step_index, incoming, handoff_store, totals):
        micro_index = 2 * last_section - step_index - section_index
        active = jnp.logical_and(micro_index >= 0, micro_index < sections)
        slot_index = jnp.clip(micro_index, 0, last_section)
        top_rows = handoff_store
        upstream = jnp.where(section_index == last_section, top_rows, incoming)
        source = lax.dynamic_index_in_dim(saved_inputs, slot_index, 0, keepdims=False)
        result, totals = lax.cond(
            active, backward_apply, backward_spare, (source, upstream, totals)
        )
        emit_rows = jnp.logical_and(active, section_index == 0)
        handoff_store = place_result(handoff_store, emit_rows, result)
        return (result, handoff_store, totals)

    def backward_turn(step_index, loop_state):
        incoming, handoff_store, totals = loop_state
        result, handoff_store, totals = backward_compute(
            step_index, incoming, handoff_store, totals
        )
        incoming = from_behind(result, "pipe", -1)
        handoff_store = from_behind(handoff_store, "pipe", 1)
        return (incoming, handoff_store, totals)

    loop_state = lax.fori_loop(0, turns - 1, backward_turn, (zero_rows, backward_store, zero_grads))
    unused, backward_store, totals = backward_compute(
        turns - 1, loop_state[0], loop_state[1], loop_state[2]
    )
    expanded = tuple((item[None] for item in totals))
    summed = (
        lax.psum_scatter(expanded[0], "dp", scatter_dimension=3, tiled=True),
        lax.psum_scatter(expanded[1], "dp", scatter_dimension=3, tiled=True),
        lax.psum_scatter(expanded[2], "dp", scatter_dimension=2, tiled=True),
        lax.psum_scatter(expanded[3], "dp", scatter_dimension=2, tiled=True),
        lax.psum_scatter(expanded[4], "dp", scatter_dimension=2, tiled=True),
        lax.psum_scatter(expanded[5], "dp", scatter_dimension=2, tiled=True),
        lax.psum_scatter(expanded[6], "dp", scatter_dimension=1, tiled=True),
    )
    factor = 1.0 / math.sqrt(micro_rows * sections * replicas)
    scaled = [item * factor for item in summed]
    return (
        forward_store,
        backward_store,
        scaled[0],
        scaled[1],
        scaled[2],
        scaled[3],
        scaled[4],
        scaled[5],
        scaled[6],
    )


def masks(ranks, count):
    rank_index = jnp.arange(count, dtype=jnp.int32)
    return (
        jnp.where(rank_index < ranks[0], 1.0, 0.0).astype(jnp.float32),
        jnp.where(rank_index < ranks[1], 1.0, 0.0).astype(jnp.float32),
    )


def parts(x):
    high = x.astype(jnp.bfloat16).astype(jnp.float32)
    return high, x - high


def dot16(a, b, ca, cb):
    return lax.dot_general(
        a.astype(jnp.bfloat16), b.astype(jnp.bfloat16), (((ca,), (cb,)), ((), ())),
        preferred_element_type=jnp.float32,
    )


def expand(a, b):
    ah, al = parts(a)
    bh, bl = parts(b)
    return dot16(jnp.concatenate([ah, al, ah], 1), jnp.concatenate([bh, bh, bl], 0), 1, 0)


def contract(a, b):
    rows, count = a.shape[0], b.shape[0]
    both = dot16(jnp.concatenate(parts(a), 0), jnp.concatenate(parts(b), 0), 1, 1)
    return both[:rows, :count] + both[:rows, count:] + both[rows:, :count]


def outer(a, b):
    ah, al = parts(a)
    bh, bl = parts(b)
    return dot16(jnp.concatenate([ah, al, ah], 0), jnp.concatenate([bh, bh, bl], 0), 0, 0)


def three(a, b, ca, cb):
    ah, al = parts(a)
    bh, bl = parts(b)
    return dot16(ah, bh, ca, cb) + dot16(ah, bl, ca, cb) + dot16(al, bh, ca, cb)


def span(index, width):
    return pl.ds(pl.multiple_of(index * width, 128), width)


def forward_kernel(
    group, pattern, rows, up_wide, down_wide, up_left, up_right, down_left, down_right, gain, masks_ref,
    out, scale_ref, low_ref, pre, low_down_ref, normed_ref, total,
):
    blocks, wide, hid = up_wide.shape
    chunk = pre.shape[1] // 16
    act = rows[...].astype(jnp.float32)
    scale = lax.rsqrt(jnp.mean(act * act, axis=1, keepdims=True) + 1e-05)
    scale_ref[...] = scale
    normed = act * scale * gain[...]
    normed_ref[...] = normed
    low = contract(normed, up_left[...]) * masks_ref[0:1, :]
    low_ref[...] = low

    def fill(i, carry):
        pre[:, span(i, chunk)] = expand(low, up_right[:, span(i, chunk)])
        return carry

    lax.fori_loop(0, 16, fill, 0)
    for k in range(blocks):
        source, target = pattern[k], pattern[blocks + k]
        pre[:, span(target, hid)] += three(normed_ref[:, span(source // group, wide)], up_wide[k], 1, 0)

    def sums(i, carry):
        return carry + contract(gelu_tanh(pre[:, span(i, chunk)]), down_left[:, span(i, chunk)])

    low_down = lax.fori_loop(0, 16, sums, jnp.zeros(low.shape, jnp.float32)) * masks_ref[1:2, :]
    low_down_ref[...] = low_down
    total[...] = act + expand(low_down, down_right[...])
    for k in range(blocks):
        source, target = pattern[2 * blocks + k], pattern[3 * blocks + k]
        part = three(gelu_tanh(pre[:, span(source, hid)]), down_wide[k], 1, 1)
        total[:, span(target // group, wide)] += part
    out[...] = total[...].astype(jnp.bfloat16)


def backward_kernel(
    group, pattern, rows, upstream, scale_ref, low_ref, pre, low_down_ref,
    up_wide, down_wide, up_left, up_right, down_left, down_right, gain, masks_ref,
    act_grad, packed, g_up, g_down, normed_ref, grad_ref, d_pre, d_normed_ref,
):
    blocks, wide, hid = up_wide.shape
    chunk = pre.shape[1] // 16
    narrow = rows.shape[1] // 16
    act = rows[...].astype(jnp.float32)
    scale = scale_ref[...]
    low = low_ref[...]
    low_down = low_down_ref[...]
    normed_ref[...] = act * scale * gain[...]
    grad_ref[...] = upstream[...].astype(jnp.float32)
    d_low_down = contract(grad_ref[...], down_right[...]) * masks_ref[1:2, :]

    def fill(i, carry):
        d_pre[:, span(i, chunk)] = expand(d_low_down, down_left[:, span(i, chunk)])
        return carry

    lax.fori_loop(0, 16, fill, 0)
    for k in range(blocks):
        source, target = pattern[2 * blocks + k], pattern[3 * blocks + k]
        piece = grad_ref[:, span(target // group, wide)]
        d_pre[:, span(source, hid)] += three(piece, down_wide[k], 1, 0)
        g_down[k] = outer(gelu_tanh(pre[:, span(source, hid)]), piece)

    def sums(i, carry):
        here = span(i, chunk)
        value = pre[:, here]
        square = value * value
        tanh = jnp.tanh(0.7978845608028654 * (value + 0.044715 * square * value))
        half = 0.5 * (1.0 + tanh)
        slope = half + 0.5 * value * (1.0 - tanh * tanh) * (
            0.7978845608028654 * (1.0 + 3.0 * 0.044715 * square)
        )
        d_here = d_pre[:, here] * slope
        d_pre[:, here] = d_here
        packed[i, :, 0:chunk] = outer(low, d_here)
        packed[i, :, chunk : 2 * chunk] = outer(d_low_down, value * half)
        return carry + contract(d_here, up_right[:, here])

    d_low = lax.fori_loop(0, 16, sums, jnp.zeros(low.shape, jnp.float32)) * masks_ref[0:1, :]
    d_normed_ref[...] = expand(d_low, up_left[...])
    for k in range(blocks):
        source, target = pattern[k], pattern[blocks + k]
        piece = d_pre[:, span(target, hid)]
        here = span(source // group, wide)
        d_normed_ref[:, here] += three(piece, up_wide[k], 1, 1)
        g_up[k] = outer(piece, normed_ref[:, here])
    d_normed = d_normed_ref[...]
    unit = act * scale
    scaled = d_normed * gain[...]
    grad = grad_ref[...]
    result = grad + scale * (scaled - unit * jnp.mean(scaled * unit, axis=1, keepdims=True))
    act_grad[...] = result.astype(jnp.bfloat16)
    g_gain = jnp.sum(d_normed * unit, axis=0, keepdims=True)
    g_up_left = outer(d_low, normed_ref[...])
    g_down_right = outer(low_down, grad)
    base = 2 * chunk
    for i in range(16):
        cut = slice(i * narrow, (i + 1) * narrow)
        packed[i, :, base : base + narrow] = g_up_left[:, cut]
        packed[i, :, base + narrow : base + 2 * narrow] = g_down_right[:, cut]
        packed[i, :, base + 2 * narrow :] = jnp.broadcast_to(g_gain[:, cut], (8, narrow))


def local_call(body, count, shapes, scratch, cost):
    vmem = pl.BlockSpec(memory_space=pltpu.VMEM)
    return pl.pallas_call(
        body,
        in_specs=[pl.BlockSpec(memory_space=pltpu.SMEM)] + [vmem] * count,
        out_specs=[vmem] * len(shapes),
        out_shape=shapes,
        scratch_shapes=scratch,
        cost_estimate=pl.CostEstimate(flops=cost, bytes_accessed=8000000, transcendentals=800000),
        compiler_params=pltpu.CompilerParams(vmem_limit_bytes=48 * 1024 * 1024),
    )


def widen(blocks, offsets, group):
    chosen = offsets[:, None] % group == jnp.arange(group)[None, :]
    wide = jnp.where(chosen[:, :, None, None], blocks[:, None], 0.0)
    return wide.reshape(blocks.shape[0], group * blocks.shape[1], blocks.shape[2])


def prepare(params, pattern, ranks):
    up_blocks, down_blocks, up_left, up_right, down_left, down_right, gain = params
    group = 4
    return (
        widen(up_blocks, pattern[0, 0], group),
        widen(down_blocks, pattern[1, 1], group),
        up_left,
        up_right,
        down_left,
        down_right,
        gain[None],
        jnp.stack(masks(ranks, up_left.shape[0])),
    )


def forward_pass(rows, ready, pattern):
    count, width = rows.shape
    rank, hidden = ready[3].shape
    f32 = jnp.float32
    shape = jax.ShapeDtypeStruct
    out, scale, low, pre, low_down = local_call(
        functools.partial(forward_kernel, 4),
        9,
        [
            shape((count, width), jnp.bfloat16),
            shape((count, 1), f32),
            shape((count, rank), f32),
            shape((count, hidden), f32),
            shape((count, rank), f32),
        ],
        [pltpu.VMEM((count, width), f32), pltpu.VMEM((count, width), f32)],
        100000000,
    )(pattern.reshape(-1), rows, *ready)
    return out, (scale, low, pre, low_down)


def backward_pass(rows, upstream, saved, ready, pattern):
    count, width = rows.shape
    rank, hidden = ready[3].shape
    blocks, wide, hid = ready[0].shape
    f32 = jnp.float32
    shape = jax.ShapeDtypeStruct
    act_grad, packed, g_up, g_down = local_call(
        functools.partial(backward_kernel, 4),
        14,
        [
            shape((count, width), jnp.bfloat16),
            shape((16, rank, (2 * hidden + 3 * width) // 16), f32),
            shape((blocks, hid, wide), f32),
            shape((blocks, hid, wide), f32),
        ],
        [
            pltpu.VMEM((count, width), f32),
            pltpu.VMEM((count, width), f32),
            pltpu.VMEM((count, hidden), f32),
            pltpu.VMEM((count, width), f32),
        ],
        200000000,
    )(pattern.reshape(-1), rows, upstream, *saved, *ready)

    return act_grad, (packed, g_up, g_down)


def pack(grads, pattern, replicas):
    packed, g_up, g_down = grads
    blocks, hid = g_up.shape[:2]

    def block_share(g, offsets):
        chosen = offsets[:, None] % 4 == jnp.arange(4)[None, :]
        cut = jnp.sum(jnp.where(chosen[:, None, :, None], g.reshape(blocks, hid, 4, -1), 0.0), axis=2)
        whole = cut.transpose(1, 0, 2).reshape(hid, -1)
        eighths = whole.reshape(replicas, -1, 8, whole.shape[1]).transpose(0, 2, 1, 3)
        return eighths.reshape(replicas, 8, -1)

    return jnp.concatenate(
        [packed, block_share(g_up, pattern[0, 0]), block_share(g_down, pattern[1, 1])], axis=2
    )


def reduce_shares(packed):
    sent = lax.all_to_all(packed.astype(jnp.bfloat16), "dp", 0, 0, tiled=True)
    return jnp.sum(sent.astype(jnp.float32), axis=0)


def two_sections(
    tokens,
    cotangent,
    norm_gain,
    up_blocks,
    down_blocks,
    up_left,
    up_right,
    down_left,
    down_right,
    block_pattern,
    rank_used,
):
    replicas = lax.axis_size("dp")
    section = lax.axis_index("pipe")
    count, width = tokens.shape
    params = (
        up_blocks[0],
        down_blocks[0],
        up_left[0],
        up_right[0],
        down_left[0],
        down_right[0],
        norm_gain[0],
    )
    pattern = block_pattern[0]
    ranks = rank_used[0]
    ready = prepare(params, pattern, ranks)
    forth, back = [(0, 1)], [(1, 0)]
    first = jnp.concatenate([tokens, lax.ppermute(tokens, "pipe", back)], axis=0)
    top = jnp.concatenate([lax.ppermute(cotangent, "pipe", forth), cotangent], axis=0)

    def run(rows):
        return forward_pass(rows, ready, pattern)

    def skip_forward(rows):
        return jax.tree.map(lambda t: jnp.zeros(t.shape, t.dtype), jax.eval_shape(run, rows))

    result, saved = lax.cond(section == 0, run, skip_forward, first)
    second = lax.ppermute(result, "pipe", forth)

    def last(operands):
        rows, upstream = operands
        out, kept = run(rows)
        below, packed = backward_pass(rows, upstream, kept, ready, pattern)
        return out, below, packed

    def skip_last(operands):
        return jax.tree.map(lambda t: jnp.zeros(t.shape, t.dtype), jax.eval_shape(last, operands))

    final, below, packed = lax.cond(section == 1, last, skip_last, (second, top))
    from_above = lax.ppermute(below, "pipe", back)
    final_early = lax.ppermute(final[:count], "pipe", back)

    def first_back(operands):
        upstream, kept, unused = operands
        return backward_pass(first, upstream, kept, ready, pattern)

    def skip_back(operands):
        return operands[0], operands[2]

    bottom, packed = lax.cond(section == 0, first_back, skip_back, (from_above, saved, packed))
    bottom_late = lax.ppermute(bottom[count:], "pipe", forth)
    final_tokens = jnp.where(section == 0, final_early, final[count:])
    input_gradient = jnp.where(section == 0, bottom[:count], bottom_late)
    factor = 1.0 / math.sqrt(count * 2 * replicas)
    share = reduce_shares(pack(packed, pattern, replicas)) * factor
    blocks, feat, hid = params[0].shape
    hidden_share = params[3].shape[1] // replicas
    width_share = width // replicas
    block_columns = hid // replicas // 8 * blocks * feat
    pieces = []
    start = 0
    for extent in (hidden_share, hidden_share, width_share, width_share, width_share, block_columns, block_columns):
        pieces.append(share[:, start : start + extent])
        start += extent

    def unpack(piece):
        rows = piece.reshape(8, -1, blocks * feat).transpose(1, 0, 2).reshape(-1, blocks, feat)
        return rows.transpose(1, 2, 0)[None]

    return (
        final_tokens,
        input_gradient,
        unpack(pieces[5]),
        unpack(pieces[6]),
        pieces[2][None],
        pieces[0][None],
        pieces[1][None],
        pieces[3][None],
        pieces[4][:1],
    )


def solution(mesh):
    body = two_sections if mesh.shape["pipe"] == 2 and mesh.shape["dp"] == 16 else shards
    return jax.shard_map(
        body,
        mesh=mesh,
        in_specs=(
            P(("pipe", "dp"), None),
            P(("pipe", "dp"), None),
            P("pipe", None),
            P("pipe", None, None, None),
            P("pipe", None, None, None),
            P("pipe", None, None),
            P("pipe", None, None),
            P("pipe", None, None),
            P("pipe", None, None),
            P("pipe", None, None, None),
            P("pipe", None),
        ),
        out_specs=(
            P(("pipe", "dp"), None),
            P(("pipe", "dp"), None),
            P("pipe", None, None, "dp"),
            P("pipe", None, None, "dp"),
            P("pipe", None, "dp"),
            P("pipe", None, "dp"),
            P("pipe", None, "dp"),
            P("pipe", None, "dp"),
            P("pipe", "dp"),
        ),
        check_vma=False,
    )
```
